32 devices in a mesh: prow: 4 (over y, x), pcol: 8 (over z, core).
Axes of the slice: x: 2, y: 2, z: 4, core: 2. Of those that a mesh axis runs over, the one named last changes fastest.
Arguments:
- window: float32 [16384, 16384], P('prow', 'pcol'), may hold values from -6 to 6
- panel: float32 [16384, 256], P(('prow', 'pcol')), may hold values from -0.046875 to 0.046875
- factor: float32 [256, 256], replicated, may hold values from -1 to 1
- col_check: float32 [16384], P('pcol'), may hold values from -6 to 6
- row_check: float32 [16384], P('prow'), may hold values from -6 to 6
Outputs:
- new_window: float32 [16384, 16384], P('prow', 'pcol')
- new_col: float32 [16384], P('pcol')
- new_row: float32 [16384], P('prow')
The draws below stay inside these ranges and needn't reach their ends.
All inputs are finite; a program needn't handle non-finite values.
Results may differ from the reference program's by a relative error of at most 0.00005.
Values sent between devices are 32-bit elements; how exact they have to be, the bound alone decides.
A program may use at most 128 MiB of HBM per device.

```python
import math
import jax
import jax.numpy as jnp
from jax import lax

N = 16384
K = 256


def level_of(stream_key, dims, shards, low, top_value):
    loudness, own = 1.0, jax.random.fold_in(stream_key, 6)
    for position, parts in shards:
        steps = jnp.exp(jax.random.uniform(jax.random.fold_in(own, position), (parts,), jnp.float32, low / len(shards), top_value / len(shards)))
        loudness = loudness * jnp.repeat(steps, dims[position] // parts).reshape([-1 if axis == position else 1 for axis in range(len(dims))])
    return loudness


def centred(stream_key, dims, scale, bound, split=(), kind=jnp.bfloat16):
    result = jax.random.normal(stream_key, dims, jnp.float32) * scale
    if len(split) > 0:
        result = level_of(stream_key, dims, split, -0.22, 0.18) * result
    return jnp.clip(result, min=-bound, max=bound).astype(kind)


def setup_inputs(seed: int = 0) -> dict:
    keys = jax.random.split(jax.random.key(seed), 6)
    window = centred(keys[0], (N, N), 1.0, 6.0, ((0, 4), (1, 8)), jnp.float32)
    panel = centred(keys[1], (N, K), N ** -0.5, 0.046875, ((0, 32),), jnp.float32)
    factor = centred(keys[2], (K, K), (1.0 / K ** 0.5), 1.0, (), jnp.float32)
    col_check = centred(keys[3], (N,), 1.0, 6.0, ((0, 8),), jnp.float32)
    row_check = centred(keys[4], (N,), 1.0, 6.0, ((0, 4),), jnp.float32)
    return {"window": window, "panel": panel, "factor": factor, "col_check": col_check, "row_check": row_check}


def unit_lower(values, row_start):
    rows = row_start + jnp.arange(values.shape[0], dtype=jnp.int32)[:, None]
    cols = jnp.arange(values.shape[1], dtype=jnp.int32)[None, :]
    ones = jnp.where(rows == cols, jnp.ones_like(values), jnp.zeros_like(values))
    return jnp.where(rows > cols, values, ones)

def reference(window, panel, factor, col_check, row_check):
    high = lax.Precision.HIGHEST
    refl = unit_lower(panel, 0)
    upper = jnp.triu(factor)
    x_prod = jnp.dot(window, refl, precision=high)
    y_prod = jnp.dot(x_prod, upper, precision=high)
    w_prod = jnp.dot(refl.T, window, precision=high)
    z_prod = jnp.dot(refl.T, y_prod, precision=high)
    m_prod = jnp.dot(upper.T, w_prod - jnp.dot(z_prod, refl.T, precision=high), precision=high)
    left = jnp.concatenate([y_prod, refl], axis=1)
    right = jnp.concatenate([refl.T, m_prod], axis=0)
    new_window = window - jnp.dot(left, right, precision=high)
    scaled = lax.optimization_barrier(jnp.sum(refl, axis=0)) / math.sqrt(N)
    col_proj = jnp.dot(col_check, refl, precision=high)
    row_proj = jnp.dot(row_check, refl, precision=high)
    new_col = col_check - jnp.dot(refl, jnp.dot(col_proj, upper, precision=high), precision=high) - jnp.dot(scaled, m_prod, precision=high)
    inner = row_proj - jnp.dot(z_prod, scaled, precision=high)
    new_row = row_check - jnp.dot(y_prod, scaled, precision=high) - jnp.dot(refl, jnp.dot(inner, upper, precision=high), precision=high)
    return (new_window, new_col, new_row)
```

```python
import functools
import math

import jax
import jax.numpy as jnp
from jax import lax
from jax.experimental import pallas as pl
from jax.experimental.pallas import tpu as pltpu
from jax.sharding import PartitionSpec as P

FULL = lax.Precision.HIGHEST
THREE = lax.Precision.HIGH


def unit_lower(values, row_start):
    rows = row_start + jnp.arange(values.shape[0], dtype=jnp.int32)[:, None]
    cols = jnp.arange(values.shape[1], dtype=jnp.int32)[None, :]
    ones = jnp.where(rows == cols, jnp.ones_like(values), jnp.zeros_like(values))
    return jnp.where(rows > cols, values, ones)


def matmul(left, right, precision=FULL):
    return jnp.dot(left, right, precision=precision)


def inner_rows(left, right, precision=FULL):
    return lax.dot_general(left, right, (((0,), (0,)), ((), ())), precision=precision)


def outer_cols(left, right, precision=FULL):
    return lax.dot_general(left, right, (((1,), (1,)), ((), ())), precision=precision)


MESH = pl.DeviceIdType.MESH


def part(ref, start, size):
    return ref.at[pl.ds(pl.multiple_of(start, 8), size)]


def remote(src, dst, send, recv, prow, pcol):
    return pltpu.make_async_remote_copy(
        src_ref=src, dst_ref=dst, send_sem=send, recv_sem=recv,
        device_id=(prow, pcol), device_id_type=MESH)


def greet(prow, pcol):
    pl.semaphore_signal(pltpu.get_barrier_semaphore(), inc=1, device_id=(prow, pcol), device_id_type=MESH)


def gather_kernel(nr, nc, panel, rows, cols, line_send, sib_send, rows_recv, move_send, move_recv, cols_send, cols_recv):
    p, c = lax.axis_index("prow"), lax.axis_index("pcol")
    pos, core, npos, size = c // 2, c % 2, nc // 2, panel.shape[0]
    sib = c + 1 - 2 * core
    flat, wanted = p * nc + c, c * nr + p
    to_p, to_c, from_p, from_c = flat % nr, flat // nr, wanted // nc, wanted % nc
    here = flat == wanted
    has_left, has_right = pos > 0, pos < npos - 1

    pl.when(has_left)(lambda: greet(p, c - 2))
    pl.when(has_right)(lambda: greet(p, c + 2))
    greet(p, sib)
    for d in range(1, nr):
        greet((p + d) % nr, c)
    pl.when(jnp.logical_not(here))(lambda: greet(from_p, from_c))
    count = has_left.astype(jnp.int32) + has_right.astype(jnp.int32) + 1 + (nr - 1) + jnp.where(here, 0, 1)
    pl.semaphore_wait(pltpu.get_barrier_semaphore(), count)

    def shard(origin):
        return part(rows, origin * size, size)

    def line(origin, slot, step):
        return remote(shard(origin), shard(origin), line_send.at[slot, origin // 2], rows_recv.at[origin], p, c + step)

    def across(origin):
        return remote(shard(origin), shard(origin), sib_send.at[origin // 2], rows_recv.at[origin], p, sib)

    rows[pl.ds(pl.multiple_of(c * size, 8), size)] = panel[...]
    mine = part(cols, p * size, size)
    move = remote(panel, part(cols, to_p * size, size), move_send, move_recv, to_p, to_c)
    pl.when(jnp.logical_not(here))(lambda: move.start())
    pl.when(has_right)(lambda: line(c, 0, 2).start())
    pl.when(has_left)(lambda: line(c, 1, -2).start())
    across(c).start()

    @pl.when(jnp.logical_not(here))
    def _():
        remote(panel, mine, move_send, move_recv, p, sib).wait_recv()

    @pl.when(here)
    def _():
        cols[pl.ds(pl.multiple_of(p * size, 8), size)] = panel[...]

    def spread(d):
        return remote(mine, mine, cols_send.at[d], cols_recv.at[p], (p + d) % nr, c)

    for d in range(1, nr):
        spread(d).start()
    for t in range(1, npos):
        @pl.when(pos >= t)
        def _():
            origin = c - 2 * t
            across(origin).wait_recv()
            pl.when(has_right)(lambda: line(origin, 0, 2).start())
            across(origin).start()

        @pl.when(pos + t < npos)
        def _():
            origin = c + 2 * t
            across(origin).wait_recv()
            pl.when(has_left)(lambda: line(origin, 1, -2).start())
            across(origin).start()
    for i in range(npos):
        across(2 * i + 1 - core).wait_recv()
    for d in range(1, nr):
        origin = (p + d) % nr
        here_part = part(cols, origin * size, size)
        remote(here_part, here_part, cols_send.at[d], cols_recv.at[origin], origin, c).wait_recv()
    for i in range(npos):
        origin = 2 * i + core
        across(origin).wait_send()
        pl.when(jnp.logical_and(has_right, i <= pos))(lambda: line(origin, 0, 2).wait_send())
        pl.when(jnp.logical_and(has_left, i >= pos))(lambda: line(origin, 1, -2).wait_send())
    for d in range(1, nr):
        spread(d).wait_send()
    pl.when(jnp.logical_not(here))(lambda: move.wait_send())


def gather(panel, nr, nc):
    size, width = panel.shape
    dma = pltpu.SemaphoreType.DMA
    vmem = pl.BlockSpec(memory_space=pltpu.VMEM)
    return pl.pallas_call(
        functools.partial(gather_kernel, nr, nc),
        out_shape=(jax.ShapeDtypeStruct((size * nc, width), panel.dtype), jax.ShapeDtypeStruct((size * nr, width), panel.dtype)),
        in_specs=[vmem],
        out_specs=(vmem, vmem),
        scratch_shapes=[dma((2, nc // 2)), dma((nc // 2,)), dma((nc,)), dma, dma, dma((nr,)), dma((nr,))],
        compiler_params=pltpu.CompilerParams(collective_id=0, has_side_effects=True, vmem_limit_bytes=32 * 2**20),
    )(panel)


def on_device(window, panel, factor, col_check, row_check):
    n_rows = lax.axis_size("prow")
    n_cols = lax.axis_size("pcol")
    prow_idx = lax.axis_index("prow")
    pcol_idx = lax.axis_index("pcol")
    rows_blk = window.shape[0]
    cols_blk = window.shape[1]
    order = rows_blk * n_rows
    upper = jnp.triu(factor)
    v_rows, v_cols = gather(panel, n_rows, n_cols)
    v_rows = unit_lower(v_rows, prow_idx * rows_blk)
    v_cols = unit_lower(v_cols, pcol_idx * cols_blk)
    col_proj, col_sums = lax.psum((matmul(col_check, v_cols), jnp.sum(v_cols, axis=0)), "pcol")
    row_part = matmul(row_check, v_rows)
    x_rows = lax.psum(matmul(window, v_cols, THREE), "pcol")
    w_trans, row_proj = lax.psum((inner_rows(window, v_rows, THREE), row_part), "prow")
    y_rows = matmul(x_rows, upper)
    coupled = lax.psum(inner_rows(v_rows, y_rows), "prow")
    m_trans = matmul(w_trans - outer_cols(v_cols, coupled), upper)
    left = jnp.concatenate([y_rows, v_rows], axis=1)
    right = jnp.concatenate([v_cols, m_trans], axis=1)
    new_window = window - outer_cols(left, right, THREE)
    scaled = col_sums / math.sqrt(order)
    new_col = col_check - matmul(v_cols, matmul(col_proj, upper)) - matmul(m_trans, scaled)
    inner = row_proj - matmul(coupled, scaled)
    new_row = row_check - matmul(y_rows, scaled) - matmul(v_rows, matmul(inner, upper))
    return (new_window, new_col, new_row)


def solution(mesh):
    placed = (P("prow", "pcol"), P(("prow", "pcol"), None), P(), P("pcol"), P("prow"))
    return jax.shard_map(
        on_device,
        mesh=mesh,
        in_specs=placed,
        out_specs=(P("prow", "pcol"), P("pcol"), P("prow")),
        check_vma=False,
    )
```
